32 devices in a mesh: grp: 2 (over y), ctx: 16 (over z, x, core).
Axes of the slice: x: 2, y: 2, z: 4, core: 2. Of those that a mesh axis runs over, the one named last changes fastest.
Arguments:
- queries: bfloat16 [4096, 4096], P(('grp', 'ctx')), parts along dimension 0, may hold values from -6 to 6
- key_matrix: bfloat16 [4096, 512], P(('grp', 'ctx')), parts along dimension 0, may hold values from -6 to 6
- value_matrix: bfloat16 [4096, 512], P(('grp', 'ctx')), parts along dimension 0, may hold values from -6 to 6
- outputs: bfloat16 [4096, 4096], P(('grp', 'ctx')), parts along dimension 0, may hold values from -6 to 6
- output_gradient: bfloat16 [4096, 4096], P(('grp', 'ctx')), parts along dimension 0, may hold values from -6 to 6
- log_normalizer: float32 [32, 4096], P(None, ('grp', 'ctx')), parts along dimension 1, may hold values from 2 to 6
- doc_lengths: int32 [16], P('grp'), parts along dimension 0, may hold values from 1 to 512, 2048 in all
Outputs:
- query_grad: bfloat16 [4096, 4096], P(('grp', 'ctx')), parts along dimension 0
- key_grad: bfloat16 [4096, 512], P(('grp', 'ctx')), parts along dimension 0
- value_grad: bfloat16 [4096, 512], P(('grp', 'ctx')), parts along dimension 0
The draws below stay inside these ranges and needn't reach their ends.
There are 2 independent parts, one for each index of `grp`. The reference program is written for one: setup_inputs(seed, part) draws one part's arguments, and reference() takes and returns one part's arrays. A program takes and returns all parts, laid end to end along the dimension named above; each array names one. Nothing has to cross between parts.
Inputs may be any that keep to these rules, and one draw needn't show every extreme that they name: `doc_lengths`: the lengths sum to 2048; the longest document has exactly 512 tokens.
All inputs are finite; a program needn't handle non-finite values.
Results may differ from the reference program's by a relative error of at most 0.0066.
Values may be sent and summed in bfloat16 or wider, within the bound.
A program may use at most 64 MiB of HBM per device.

```python
import math
import jax
import jax.numpy as jnp
import numpy as np
from jax import lax

KEY_VALUE_HEADS = 4
HEAD_SIZE = 128
QUERY_HEADS = 32
SHARD_TOKENS = 128
SPAN = 4
MOST = 512
WINDOW_TOKENS = 2048
DOCS = 8
N_CTX = 16


def shard_levels(key, dims, split, least, largest):
    def one(dim, shards_of):
        draws = jax.random.uniform(jax.random.fold_in(jax.random.fold_in(key, 6), dim), (shards_of,), jnp.float32, least / len(split), largest / len(split))
        return jnp.repeat(jnp.exp(draws), dims[dim] // shards_of).reshape((-1,) + (1,) * (len(dims) - dim - 1))

    factor_of = one(*split[0])
    for cut in split[1:]:
        factor_of = factor_of * one(*cut)
    return factor_of


def split_up(amount, total, reach, skew):
    portions = [(1 << 20) // math.isqrt(grade ** skew) + 1 for grade in range(2, amount + 1)]
    surplus, counts = total - reach - (amount - 1), [1] * (amount - 1)
    while surplus > 0:
        movable = [i for i in range(amount - 1) if counts[i] < reach]
        mass, budget = sum([portions[i] for i in movable]), surplus
        for i in movable:
            more = min(reach - counts[i], max(1, budget * portions[i] // mass), surplus)
            counts[i] = counts[i] + more
            surplus = surplus - more
    return np.array([reach] + counts)


def ragged_sizes(own_key, amount, total, limit, lean):
    if amount == 2:
        one = jax.random.randint(own_key, (), max(1, total - limit), min(limit, total - 1) + 1)
        return jnp.stack([one, total - one])
    sizes = jnp.asarray(split_up(amount, total, limit, lean), jnp.int32)
    couples = (amount - 1) // 2
    donor, receiver = sizes[1:1 + 2 * couples:2], sizes[2:2 + 2 * couples:2]
    room = jnp.minimum(donor - 1, limit - receiver)
    passed = jax.random.randint(jax.random.fold_in(own_key, 1), (couples,), 0, 1 << 20) % (room + 1)
    sizes = sizes.at[1:1 + 2 * couples:2].set(donor - passed).at[2:2 + 2 * couples:2].set(receiver + passed)
    return sizes[jax.random.permutation(jax.random.fold_in(own_key, 2), amount)]


def gaussian(rng, dims, spread, limit, pieces=(), kind=jnp.bfloat16):
    drawn = spread * jax.random.normal(rng, dims, jnp.float32)
    if pieces:
        drawn = drawn * shard_levels(rng, dims, pieces, -0.22, 0.18)
    return jnp.clip(drawn, -limit, limit).astype(kind)


def setup_inputs(seed: int = 0, part: int = 0) -> dict:
    arg_keys = jax.random.split(jax.random.key(seed), 8)
    part_keys = jax.random.split(jax.random.fold_in(arg_keys[7], part), 8)
    return {
        "queries": gaussian(part_keys[0], (WINDOW_TOKENS, QUERY_HEADS * HEAD_SIZE), 1.0, 6.0, ((0, 16),)),
        "key_matrix": gaussian(part_keys[1], (WINDOW_TOKENS, KEY_VALUE_HEADS * HEAD_SIZE), 1.0, 6.0, ((0, 16),)),
        "value_matrix": gaussian(part_keys[2], (WINDOW_TOKENS, KEY_VALUE_HEADS * HEAD_SIZE), 1.0, 6.0, ((0, 16),)),
        "outputs": gaussian(part_keys[3], (WINDOW_TOKENS, QUERY_HEADS * HEAD_SIZE), 1.0, 6.0, ((0, 16),)),
        "output_gradient": gaussian(part_keys[4], (WINDOW_TOKENS, QUERY_HEADS * HEAD_SIZE), 1.0, 6.0, ((0, 16),)),
        "log_normalizer": jnp.clip(2.0 + 4.0 * jax.random.uniform(part_keys[5], (QUERY_HEADS, WINDOW_TOKENS), jnp.float32) ** shard_levels(part_keys[5], (QUERY_HEADS, WINDOW_TOKENS), ((1, 16),), -0.2, 0.2), 2.0, 6.0),
        "doc_lengths": ragged_sizes(part_keys[6], DOCS, WINDOW_TOKENS, MOST, 2).astype(jnp.int32),
    }


def doc_index(doc_lengths, positions):
    doc_ends = jnp.cumsum(doc_lengths)
    return lax.optimization_barrier(jnp.sum((positions[:, None] >= doc_ends[None, :]).astype(jnp.int32), axis=1))

def reference(queries, key_matrix, value_matrix, outputs, output_gradient, log_normalizer, doc_lengths):
    inv_root = 1.0 / math.sqrt(HEAD_SIZE)
    margin = SPAN * SHARD_TOKENS
    tile_width = margin + SHARD_TOKENS
    head_group = QUERY_HEADS // KEY_VALUE_HEADS
    key_value_columns = KEY_VALUE_HEADS * HEAD_SIZE
    key_with_padding = jnp.concatenate([jnp.zeros((margin, key_value_columns), key_matrix.dtype), key_matrix], axis=0)
    value_with_padding = jnp.concatenate([jnp.zeros((margin, key_value_columns), value_matrix.dtype), value_matrix], axis=0)

    def step(totals, block):
        key_total, value_total = totals
        first_row_index = (block * SHARD_TOKENS).astype(jnp.int32)
        query_tile = lax.dynamic_slice_in_dim(queries, first_row_index, SHARD_TOKENS, 0).astype(jnp.float32).reshape(SHARD_TOKENS, KEY_VALUE_HEADS, head_group, HEAD_SIZE)
        output_tile = lax.dynamic_slice_in_dim(outputs, first_row_index, SHARD_TOKENS, 0).astype(jnp.float32).reshape(SHARD_TOKENS, KEY_VALUE_HEADS, head_group, HEAD_SIZE)
        gradient_tile = lax.dynamic_slice_in_dim(output_gradient, first_row_index, SHARD_TOKENS, 0).astype(jnp.float32).reshape(SHARD_TOKENS, KEY_VALUE_HEADS, head_group, HEAD_SIZE)
        key_tile = lax.dynamic_slice_in_dim(key_with_padding, first_row_index, tile_width, 0).astype(jnp.float32).reshape(tile_width, KEY_VALUE_HEADS, HEAD_SIZE)
        value_tile = lax.dynamic_slice_in_dim(value_with_padding, first_row_index, tile_width, 0).astype(jnp.float32).reshape(tile_width, KEY_VALUE_HEADS, HEAD_SIZE)
        normalizer_tile = lax.dynamic_slice_in_dim(log_normalizer, first_row_index, SHARD_TOKENS, 1).reshape(KEY_VALUE_HEADS, head_group, SHARD_TOKENS, 1)
        query_pos = first_row_index + jnp.arange(SHARD_TOKENS, dtype=jnp.int32)
        key_pos = first_row_index - margin + jnp.arange(tile_width, dtype=jnp.int32)
        allowed = (key_pos[None, :] <= query_pos[:, None]) & (key_pos[None, :] >= 0)
        allowed = allowed & (doc_index(doc_lengths, query_pos)[:, None] == doc_index(doc_lengths, key_pos)[None, :])
        scores = jnp.einsum('tkgd,skd->kgts', query_tile, key_tile) * inv_root
        weights = jnp.where(allowed, jnp.exp(scores - normalizer_tile), 0.0)
        weights_low = weights.astype(jnp.bfloat16).astype(jnp.float32)
        row_dot = jnp.transpose(lax.optimization_barrier(jnp.sum(gradient_tile * output_tile, axis=3)), (1, 2, 0))
        grad_prob = jnp.einsum('tkgd,skd->kgts', gradient_tile, value_tile)
        grad_score = (weights * (grad_prob - row_dot[..., None]) * inv_root).astype(jnp.bfloat16).astype(jnp.float32)
        query_part = jnp.einsum('kgts,skd->tkgd', grad_score, key_tile).reshape(SHARD_TOKENS, QUERY_HEADS * HEAD_SIZE)
        key_part = jnp.einsum('kgts,tkgd->skd', grad_score, query_tile).reshape(tile_width, key_value_columns)
        value_part = jnp.einsum('kgts,tkgd->skd', weights_low, gradient_tile).reshape(tile_width, key_value_columns)
        key_total = lax.dynamic_update_slice_in_dim(key_total, lax.dynamic_slice_in_dim(key_total, first_row_index, tile_width, 0) + key_part, first_row_index, 0)
        value_total = lax.dynamic_update_slice_in_dim(value_total, lax.dynamic_slice_in_dim(value_total, first_row_index, tile_width, 0) + value_part, first_row_index, 0)
        return ((key_total, value_total), query_part.astype(jnp.bfloat16))
    start_totals = (jnp.zeros((WINDOW_TOKENS + margin, key_value_columns), jnp.float32), jnp.zeros((WINDOW_TOKENS + margin, key_value_columns), jnp.float32))
    (key_total, value_total), query_blocks = lax.scan(step, start_totals, jnp.arange(N_CTX, dtype=jnp.int32))
    query_grad = query_blocks.reshape(WINDOW_TOKENS, QUERY_HEADS * HEAD_SIZE)
    return (query_grad, key_total[margin:].astype(jnp.bfloat16), value_total[margin:].astype(jnp.bfloat16))
```

```python
import functools
import math

import jax
import jax.numpy as jnp
from jax import lax
from jax.experimental import pallas as pl
from jax.experimental.pallas import tpu as pltpu
from jax.sharding import PartitionSpec as P

HD = 128
KVH = 4
SPAN = 4
LOG2E = 1.0 / math.log(2.0)
MESH = pl.DeviceIdType.MESH
F32 = jnp.float32
BF16 = jnp.bfloat16

CX, C, X, PB, M = range(5)


def nt(a, b):
    return lax.dot_general(a, b, (((1,), (1,)), ((), ())), preferred_element_type=F32)


def nn(a, b):
    return jnp.dot(a, b, preferred_element_type=F32)


def kernel(
    n, docs,
    doc_ref, q_hbm, k_hbm, v_hbm, o_hbm, do_hbm, ln_hbm,
    dq_hbm, dk_ref, dv_ref,
    q, o, do, ln, own, dq, kv, bias, rd, wbuf, gbuf, kt, acc_x, acc, bsend, brecv,
    load_sem, store_sem, fs_sem, fr_sem, bs_sem, br_sem,
):
    T = q_hbm.shape[0]
    heads = q_hbm.shape[1] // HD
    group = heads // KVH
    wide = group * HD
    inv_root = 1.0 / math.sqrt(HD)
    me = lax.axis_index("ctx")
    place = lax.rem(me, 4)
    x = place // 2
    c = lax.rem(place, 2)
    mate = me + 1 - 2 * c
    peer = me + 2 - 4 * x
    after = me + SPAN
    before = me - SPAN
    has_after = after < n
    has_before = before >= 0

    def load(i, src, dst):
        return pltpu.make_async_copy(src, dst, load_sem.at[i])

    loads_kv = [load(0, k_hbm, own.at[0]), load(1, v_hbm, own.at[1])]
    loads_rd = [load(2, do_hbm, do), load(3, o_hbm, o)]
    loads_q = [load(4, q_hbm, q), load(5, ln_hbm, ln)]
    for cp in loads_kv + loads_rd + loads_q:
        cp.start()

    barrier = pltpu.get_barrier_semaphore()
    pl.semaphore_signal(barrier, inc=1, device_id={"ctx": mate}, device_id_type=MESH)
    pl.semaphore_signal(barrier, inc=1, device_id={"ctx": peer}, device_id_type=MESH)

    @pl.when(has_after)
    def _():
        pl.semaphore_signal(barrier, inc=1, device_id={"ctx": after}, device_id_type=MESH)

    @pl.when(has_before)
    def _():
        pl.semaphore_signal(barrier, inc=1, device_id={"ctx": before}, device_id_type=MESH)

    for cp in loads_kv:
        cp.wait()
    for g in range(KVH):
        for a in range(2):
            kv[g, a, M * T:(M + 1) * T, :] = own[a, :, g * HD:(g + 1) * HD]

    @pl.when(jnp.logical_not(has_before))
    def _():
        kv[:, :, PB * T:(PB + 1) * T, :] = jnp.zeros((KVH, 2, T, HD), BF16)

    wait_for = 2 + jnp.where(has_after, 1, 0) + jnp.where(has_before, 1, 0)
    pl.semaphore_wait(barrier, wait_for)

    def fwd(kind, g, slot, target):
        row = slot * T if isinstance(slot, int) else pl.multiple_of(slot * T, T)
        return pltpu.make_async_remote_copy(
            src_ref=kv.at[g, :, pl.ds(row, T), :],
            dst_ref=kv.at[g, :, pl.ds(kind * T, T), :],
            send_sem=fs_sem.at[kind, g], recv_sem=fr_sem.at[kind, g],
            device_id={"ctx": target}, device_id_type=MESH,
        )

    def fwd_p(g):
        return fwd(PB, g, M, after)

    def fwd_x(g):
        return fwd(X, g, M - x, peer)

    def fwd_c(g):
        return fwd(C, g, M - c, mate)

    def fwd_cx(g):
        return fwd(CX, g, X, mate)

    @pl.when(has_after)
    def _():
        for g in range(KVH):
            fwd_p(g).start()

    @pl.when(x == 0)
    def _():
        for g in range(KVH):
            fwd_x(g).start()

    @pl.when(c == 0)
    def _():
        for g in range(KVH):
            fwd_c(g).start()

    def relay_p(g):
        @pl.when(has_before)
        def _():
            fwd_p(g).wait_recv()

        @pl.when(x == 1)
        def _():
            fwd_x(g).start()

        @pl.when(c == 1)
        def _():
            fwd_c(g).start()

    def relay_x(g):
        fwd_x(g).wait_recv()
        fwd_cx(g).start()

    def arrived(g):
        fwd_c(g).wait_recv()
        fwd_cx(g).wait_recv()

    t_row = lax.broadcasted_iota(jnp.int32, (1, T), 1)
    pos_row = me * T + t_row
    start_row = jnp.zeros((1, T), jnp.int32)
    end = jnp.int32(0)
    for i in range(docs):
        end = end + doc_ref[i]
        start_row = jnp.where(end <= pos_row, jnp.maximum(start_row, end), start_row)
    s_col = lax.broadcasted_iota(jnp.int32, (T, T), 0)
    t_col = lax.broadcasted_iota(jnp.int32, (T, T), 1)
    tri1 = s_col <= t_col
    bases = (me - 1 - 2 * c, me - 3 + 2 * c, me - 2)
    for slot, base in enumerate(bases):
        ok = base * T + s_col >= start_row
        b = jnp.where(ok, 0.0, -1e30).astype(F32)
        bias[slot * T:(slot + 1) * T, :] = b
    ok = jnp.where(tri1, me, me - SPAN) * T + s_col >= start_row
    bias[3 * T:4 * T, :] = jnp.where(ok, 0.0, -1e30).astype(F32)

    for cp in loads_rd:
        cp.wait()
    pick = (
        lax.broadcasted_iota(jnp.int32, (16, wide), 1) // HD
        == lax.broadcasted_iota(jnp.int32, (16, wide), 0)
    )
    ones = jnp.where(pick, 1.0, 0.0).astype(BF16)
    for g in range(KVH):
        cols = slice(g * wide, (g + 1) * wide)
        prod = do[:, cols].astype(F32) * o[:, cols].astype(F32)
        high = prod.astype(BF16)
        low = (prod - high.astype(F32)).astype(BF16)
        rd[g * group:(g + 1) * group, :] = (nt(ones, high) + nt(ones, low))[:group]
    for cp in loads_q:
        cp.wait()

    relay_p(0)
    relay_x(0)
    relay_p(1)

    def bwd(kind, g, target):
        return pltpu.make_async_remote_copy(
            src_ref=bsend.at[kind, g], dst_ref=brecv.at[kind, g],
            send_sem=bs_sem.at[kind, g], recv_sem=br_sem.at[kind, g],
            device_id={"ctx": target}, device_id_type=MESH,
        )

    def store(g):
        cols = pl.ds(g * wide, wide)
        return pltpu.make_async_copy(dq.at[:, cols], dq_hbm.at[:, cols], store_sem.at[g])

    def hop2(g):
        bwd(CX, g, mate).wait_recv()
        bsend[X, g] = (acc_x[g] + brecv[CX, g].astype(F32)).astype(BF16)
        bwd(X, g, peer).start()

    def hop3(g):
        bwd(C, g, mate).wait_recv()
        acc[c, g] = acc[c, g] + brecv[C, g].astype(F32)
        bwd(X, g, peer).wait_recv()
        acc[x, g] = acc[x, g] + brecv[X, g].astype(F32)

        @pl.when(has_before)
        def _():
            bsend[PB, g] = acc[1, g].astype(BF16)
            bwd(PB, g, before).start()

    def hop4(g):
        cols = slice(g * HD, (g + 1) * HD)

        @pl.when(has_after)
        def _():
            bwd(PB, g, before).wait_recv()
            total = acc[0, g] + brecv[PB, g].astype(F32)
            dk_ref[:, cols] = total[0].astype(BF16)
            dv_ref[:, cols] = total[1].astype(BF16)

        @pl.when(jnp.logical_not(has_after))
        def _():
            dk_ref[:, cols] = acc[0, g, 0].astype(BF16)
            dv_ref[:, cols] = acc[0, g, 1].astype(BF16)

    def pair_rows(ref, h):
        return jnp.concatenate(
            [ref[:, h * HD:(h + 1) * HD], ref[:, (h + 1) * HD:(h + 2) * HD]], axis=0
        )

    def pair_lanes(ref, h):
        return jnp.concatenate([ref[h:h + 1, :], ref[h + 1:h + 2, :]], axis=1)

    def scores(g, between):
        k_all = kv[g, 0]
        v_all = kv[g, 1]
        kt[...] = k_all.T
        tri = jnp.concatenate([tri1, tri1], axis=1)
        for p in range(group // 2):
            h = g * group + 2 * p
            st = nt(k_all, pair_rows(q, h))
            gp = nt(v_all, pair_rows(do, h))
            shift = pair_lanes(ln, h) * LOG2E
            dot_row = pair_lanes(rd, h)
            lanes = slice(p * 2 * T, (p + 1) * 2 * T)
            for slot in range(4):
                rows = slice(slot * T, (slot + 1) * T)
                s_t, g_t = st[rows], gp[rows]
                if slot == 3:
                    s_t = jnp.where(tri, st[M * T:], s_t)
                    g_t = jnp.where(tri, gp[M * T:], g_t)
                b = bias[rows, :]
                b = jnp.concatenate([b, b], axis=1)
                w = jnp.exp2(s_t * (inv_root * LOG2E) - shift + b)
                gs = w * (g_t - dot_row)
                if slot == 3:
                    wbuf[M * T:, lanes] = jnp.where(tri, w, 0.0).astype(BF16)
                    gbuf[M * T:, lanes] = jnp.where(tri, gs, 0.0).astype(BF16)
                    w = jnp.where(tri, 0.0, w)
                    gs = jnp.where(tri, 0.0, gs)
                wbuf[rows, lanes] = w.astype(BF16)
                gbuf[rows, lanes] = gs.astype(BF16)
            dqt = nn(kt[...], gbuf[:, lanes]) * inv_root
            dq[:, h * HD:(h + 1) * HD] = dqt[:, :T].T.astype(BF16)
            dq[:, (h + 1) * HD:(h + 2) * HD] = dqt[:, T:].T.astype(BF16)
            between(p)

    def stacked(ref, g):
        return jnp.concatenate(
            [ref[:, (g * group + i) * HD:(g * group + i + 1) * HD] for i in range(group)], axis=0
        )

    for g in range(KVH):
        if g > 0:
            relay_x(g)
            if g + 1 < KVH:
                relay_p(g + 1)
        arrived(g)

        def between(p, g=g):
            if p == 1 and g >= 1:
                hop2(g - 1)
            if p == 3 and g >= 1:
                hop3(g - 1)

        scores(g, between)
        store(g).start()
        dk = nn(gbuf[...], stacked(q, g)) * inv_root
        dv = nn(wbuf[...], stacked(do, g))
        for kind in (CX, C):
            bsend[kind, g, 0] = dk[kind * T:(kind + 1) * T].astype(BF16)
            bsend[kind, g, 1] = dv[kind * T:(kind + 1) * T].astype(BF16)
            bwd(kind, g, mate).start()
        for a, part in enumerate((dk, dv)):
            acc_x[g, a] = part[X * T:(X + 1) * T]
            acc[1, g, a] = part[PB * T:(PB + 1) * T]
            acc[0, g, a] = part[M * T:]
    hop2(KVH - 1)
    for g in range(KVH - 1):
        hop4(g)
    hop3(KVH - 1)
    hop4(KVH - 1)

    for g in range(KVH):
        store(g).wait()
        for kind, target in ((CX, mate), (C, mate), (X, peer)):
            bwd(kind, g, target).wait_send()
        fwd_x(g).wait_send()
        fwd_c(g).wait_send()
        fwd_cx(g).wait_send()

    @pl.when(has_after)
    def _():
        for g in range(KVH):
            fwd_p(g).wait_send()

    @pl.when(has_before)
    def _():
        for g in range(KVH):
            bwd(PB, g, before).wait_send()


def body(n, queries, keys, values, outputs, out_grad, log_normalizer, doc_lengths):
    T, width = queries.shape
    heads = width // HD
    group = heads // KVH
    any_spec = pl.BlockSpec(memory_space=pl.ANY)
    vmem = pl.BlockSpec(memory_space=pltpu.VMEM)
    dma = pltpu.SemaphoreType.DMA
    return pl.pallas_call(
        functools.partial(kernel, n, doc_lengths.shape[0]),
        out_shape=(
            jax.ShapeDtypeStruct(queries.shape, BF16),
            jax.ShapeDtypeStruct(keys.shape, BF16),
            jax.ShapeDtypeStruct(values.shape, BF16),
        ),
        in_specs=[pl.BlockSpec(memory_space=pltpu.SMEM)] + [any_spec] * 6,
        out_specs=(any_spec, vmem, vmem),
        scratch_shapes=[
            pltpu.VMEM((T, width), BF16),
            pltpu.VMEM((T, width), BF16),
            pltpu.VMEM((T, width), BF16),
            pltpu.VMEM((heads, T), F32),
            pltpu.VMEM((2, T, KVH * HD), BF16),
            pltpu.VMEM((T, width), BF16),
            pltpu.VMEM((KVH, 2, 5 * T, HD), BF16),
            pltpu.VMEM((4 * T, T), F32),
            pltpu.VMEM((heads, T), F32),
            pltpu.VMEM((5 * T, group * T), BF16),
            pltpu.VMEM((5 * T, group * T), BF16),
            pltpu.VMEM((HD, 5 * T), BF16),
            pltpu.VMEM((KVH, 2, T, HD), F32),
            pltpu.VMEM((2, KVH, 2, T, HD), F32),
            pltpu.VMEM((4, KVH, 2, T, HD), BF16),
            pltpu.VMEM((4, KVH, 2, T, HD), BF16),
            dma((6,)), dma((KVH,)),
            dma((4, KVH)), dma((4, KVH)), dma((4, KVH)), dma((4, KVH)),
        ],
        compiler_params=pltpu.CompilerParams(
            collective_id=0, has_side_effects=True, vmem_limit_bytes=40 * 1024 * 1024
        ),
        name="attention_grad",
    )(doc_lengths, queries, keys, values, outputs, out_grad, log_normalizer)


def solution(mesh):
    rows = P(("grp", "ctx"), None)
    in_specs = (rows,) * 5 + (P(None, ("grp", "ctx")), P("grp"))
    return jax.shard_map(
        functools.partial(body, mesh.shape["ctx"]),
        mesh=mesh, in_specs=in_specs, out_specs=(rows,) * 3, check_vma=False,
    )
```

```python
import functools
import math

import jax
import jax.numpy as jnp
from jax import lax
from jax.experimental import pallas as pl
from jax.experimental.pallas import tpu as pltpu
from jax.sharding import PartitionSpec as P

HD = 128
KVH = 4
SPAN = 4
LOG2E = 1.0 / math.log(2.0)
MESH = pl.DeviceIdType.MESH
F32 = jnp.float32
BF16 = jnp.bfloat16

CX, C, X, PB, M = range(5)


def nt(a, b):
    return lax.dot_general(a, b, (((1,), (1,)), ((), ())), preferred_element_type=F32)


def nn(a, b):
    return jnp.dot(a, b, preferred_element_type=F32)


def kernel(
    n, docs,
    doc_ref, q_hbm, k_hbm, v_hbm, o_hbm, do_hbm, ln_hbm,
    dq_hbm, dk_ref, dv_ref,
    q, o, do, ln, own, dq, dq_sum, kv, bias, rd, wbuf, gbuf, kt, acc_x, acc, bsend, brecv,
    load_sem, store_sem, fs_sem, fr_sem, bs_sem, br_sem,
):
    T = q_hbm.shape[0]
    heads = q_hbm.shape[1] // HD
    group = heads // KVH
    wide = group * HD
    inv_root = 1.0 / math.sqrt(HD)
    me = lax.axis_index("ctx")
    place = lax.rem(me, 4)
    x = place // 2
    c = lax.rem(place, 2)
    mate = me + 1 - 2 * c
    peer = me + 2 - 4 * x
    after = me + SPAN
    before = me - SPAN
    has_after = after < n
    has_before = before >= 0

    def load(i, src, dst):
        return pltpu.make_async_copy(src, dst, load_sem.at[i])

    loads_kv = [load(0, k_hbm, own.at[0]), load(1, v_hbm, own.at[1])]
    loads_rd = [load(2, do_hbm, do), load(3, o_hbm, o)]
    loads_q = [load(4, q_hbm, q), load(5, ln_hbm, ln)]
    for cp in loads_kv + loads_rd + loads_q:
        cp.start()

    barrier = pltpu.get_barrier_semaphore()
    pl.semaphore_signal(barrier, inc=1, device_id={"ctx": mate}, device_id_type=MESH)
    pl.semaphore_signal(barrier, inc=1, device_id={"ctx": peer}, device_id_type=MESH)

    @pl.when(has_after)
    def _():
        pl.semaphore_signal(barrier, inc=1, device_id={"ctx": after}, device_id_type=MESH)

    @pl.when(has_before)
    def _():
        pl.semaphore_signal(barrier, inc=1, device_id={"ctx": before}, device_id_type=MESH)

    for cp in loads_kv:
        cp.wait()
    for g in range(KVH):
        for a in range(2):
            kv[g, a, M * T:(M + 1) * T, :] = own[a, :, g * HD:(g + 1) * HD]

    @pl.when(jnp.logical_not(has_before))
    def _():
        kv[:, :, PB * T:(PB + 1) * T, :] = jnp.zeros((KVH, 2, T, HD), BF16)

    wait_for = 2 + jnp.where(has_after, 1, 0) + jnp.where(has_before, 1, 0)
    pl.semaphore_wait(barrier, wait_for)

    def fwd(kind, g, slot, target):
        row = slot * T if isinstance(slot, int) else pl.multiple_of(slot * T, T)
        return pltpu.make_async_remote_copy(
            src_ref=kv.at[g, :, pl.ds(row, T), :],
            dst_ref=kv.at[g, :, pl.ds(kind * T, T), :],
            send_sem=fs_sem.at[kind, g], recv_sem=fr_sem.at[kind, g],
            device_id={"ctx": target}, device_id_type=MESH,
        )

    def fwd_p(g):
        return fwd(PB, g, M, after)

    def fwd_x(g):
        return fwd(X, g, M - x, peer)

    def fwd_c(g):
        return fwd(C, g, M - c, mate)

    def fwd_cx(g):
        return fwd(CX, g, X, mate)

    @pl.when(has_after)
    def _():
        for g in range(KVH):
            fwd_p(g).start()

    @pl.when(x == 0)
    def _():
        for g in range(KVH):
            fwd_x(g).start()

    @pl.when(c == 0)
    def _():
        for g in range(KVH):
            fwd_c(g).start()

    def relay_p(g):
        @pl.when(has_before)
        def _():
            fwd_p(g).wait_recv()

        @pl.when(x == 1)
        def _():
            fwd_x(g).start()

        @pl.when(c == 1)
        def _():
            fwd_c(g).start()

    def relay_x(g):
        fwd_x(g).wait_recv()
        fwd_cx(g).start()

    def arrived(g):
        fwd_c(g).wait_recv()
        fwd_cx(g).wait_recv()

    t_row = lax.broadcasted_iota(jnp.int32, (1, T), 1)
    pos_row = me * T + t_row
    start_row = jnp.zeros((1, T), jnp.int32)
    end = jnp.int32(0)
    for i in range(docs):
        end = end + doc_ref[i]
        start_row = jnp.where(end <= pos_row, jnp.maximum(start_row, end), start_row)
    s_col = lax.broadcasted_iota(jnp.int32, (T, T), 0)
    t_col = lax.broadcasted_iota(jnp.int32, (T, T), 1)
    bases = (me - 1 - 2 * c, me - 3 + 2 * c, me - 2, me - SPAN, me)
    for slot, base in enumerate(bases):
        ok = base * T + s_col >= start_row
        if slot == PB:
            ok = ok & (s_col > t_col)
        if slot == M:
            ok = ok & (s_col <= t_col)
        bias[slot * T:(slot + 1) * T, :] = jnp.where(ok, 0.0, -1e30).astype(F32)

    for cp in loads_rd:
        cp.wait()
    pick = (
        lax.broadcasted_iota(jnp.int32, (16, wide), 1) // HD
        == lax.broadcasted_iota(jnp.int32, (16, wide), 0)
    )
    ones = jnp.where(pick, 1.0, 0.0).astype(BF16)
    for g in range(KVH):
        cols = slice(g * wide, (g + 1) * wide)
        prod = do[:, cols].astype(F32) * o[:, cols].astype(F32)
        high = prod.astype(BF16)
        low = (prod - high.astype(F32)).astype(BF16)
        rd[g * group:(g + 1) * group, :] = (nt(ones, high) + nt(ones, low))[:group]
    for cp in loads_q:
        cp.wait()

    def bwd(kind, g, target):
        return pltpu.make_async_remote_copy(
            src_ref=bsend.at[kind, g], dst_ref=brecv.at[kind, g],
            send_sem=bs_sem.at[kind, g], recv_sem=br_sem.at[kind, g],
            device_id={"ctx": target}, device_id_type=MESH,
        )

    def store(g):
        cols = pl.ds(g * wide, wide)
        return pltpu.make_async_copy(dq.at[:, cols], dq_hbm.at[:, cols], store_sem.at[g])

    def hop2(g):
        bwd(CX, g, mate).wait_recv()
        bsend[X, g] = (acc_x[g] + brecv[CX, g].astype(F32)).astype(BF16)
        bwd(X, g, peer).start()

    def hop3(g):
        bwd(C, g, mate).wait_recv()
        acc[c, g] = acc[c, g] + brecv[C, g].astype(F32)
        bwd(X, g, peer).wait_recv()
        acc[x, g] = acc[x, g] + brecv[X, g].astype(F32)

        @pl.when(has_before)
        def _():
            bsend[PB, g] = acc[1, g].astype(BF16)
            bwd(PB, g, before).start()

    def hop4(g):
        cols = slice(g * HD, (g + 1) * HD)

        @pl.when(has_after)
        def _():
            bwd(PB, g, before).wait_recv()
            total = acc[0, g] + brecv[PB, g].astype(F32)
            dk_ref[:, cols] = total[0].astype(BF16)
            dv_ref[:, cols] = total[1].astype(BF16)

        @pl.when(jnp.logical_not(has_after))
        def _():
            dk_ref[:, cols] = acc[0, g, 0].astype(BF16)
            dv_ref[:, cols] = acc[0, g, 1].astype(BF16)

    def pair_rows(ref, h):
        return jnp.concatenate(
            [ref[:, h * HD:(h + 1) * HD], ref[:, (h + 1) * HD:(h + 2) * HD]], axis=0
        )

    def pair_lanes(ref, h):
        return jnp.concatenate([ref[h:h + 1, :], ref[h + 1:h + 2, :]], axis=1)

    def tiles(g, first, last, start_sum, between=None):
        rows = slice(first * T, (last + 1) * T)
        k_rows = kv[g, 0, rows, :]
        v_rows = kv[g, 1, rows, :]
        kt[:, rows] = k_rows.T
        for p in range(group // 2):
            h = g * group + 2 * p
            st = nt(k_rows, pair_rows(q, h))
            gp = nt(v_rows, pair_rows(do, h))
            shift = pair_lanes(ln, h) * LOG2E
            dot_row = pair_lanes(rd, h)
            lanes = slice(p * 2 * T, (p + 1) * 2 * T)
            for slot in range(first, last + 1):
                part = slice((slot - first) * T, (slot - first + 1) * T)
                here = slice(slot * T, (slot + 1) * T)
                b = bias[here, :]
                b = jnp.concatenate([b, b], axis=1)
                w = jnp.exp2(st[part] * (inv_root * LOG2E) - shift + b)
                gs = w * (gp[part] - dot_row)
                wbuf[here, lanes] = w.astype(BF16)
                gbuf[here, lanes] = gs.astype(BF16)
            dqt = nn(kt[:, rows], gbuf[rows, lanes])
            sums = slice(h * T, (h + 2) * T)
            if start_sum:
                dq_sum[:, sums] = dqt
            elif last != PB:
                dq_sum[:, sums] += dqt
            else:
                dqt = (dq_sum[:, sums] + dqt) * inv_root
                dq[:, h * HD:(h + 1) * HD] = dqt[:, :T].T.astype(BF16)
                dq[:, (h + 1) * HD:(h + 2) * HD] = dqt[:, T:].T.astype(BF16)
            if between is not None:
                between(p)
        dk = nn(gbuf[rows, :], stacked(q, g)) * inv_root
        dv = nn(wbuf[rows, :], stacked(do, g))
        return dk, dv

    def stacked(ref, g):
        return jnp.concatenate(
            [ref[:, (g * group + i) * HD:(g * group + i + 1) * HD] for i in range(group)], axis=0
        )

    for g in range(KVH):
        for a, part in enumerate(tiles(g, M, M, True)):
            acc[0, g, a] = part
        relay_p(g)

    relay_x(0)
    relay_x(1)
    for g in range(KVH):
        arrived(g)

        def between(p, g=g):
            if p == 0 and g + 2 < KVH:
                relay_x(g + 2)
            if p == 3 and g >= 1:
                hop2(g - 1)

        dk, dv = tiles(g, CX, X, False, between)
        for kind in (CX, C):
            bsend[kind, g, 0] = dk[kind * T:(kind + 1) * T].astype(BF16)
            bsend[kind, g, 1] = dv[kind * T:(kind + 1) * T].astype(BF16)
            bwd(kind, g, mate).start()
        acc_x[g, 0] = dk[X * T:]
        acc_x[g, 1] = dv[X * T:]

    for g in range(KVH):
        for a, part in enumerate(tiles(g, PB, PB, False)):
            acc[1, g, a] = part
        store(g).start()
        if g == 0:
            hop2(KVH - 1)
        hop3(g)
    for g in range(KVH):
        hop4(g)

    for g in range(KVH):
        store(g).wait()
        for kind, target in ((CX, mate), (C, mate), (X, peer)):
            bwd(kind, g, target).wait_send()
        fwd_x(g).wait_send()
        fwd_c(g).wait_send()
        fwd_cx(g).wait_send()

    @pl.when(has_after)
    def _():
        for g in range(KVH):
            fwd_p(g).wait_send()

    @pl.when(has_before)
    def _():
        for g in range(KVH):
            bwd(PB, g, before).wait_send()


def body(n, queries, keys, values, outputs, out_grad, log_normalizer, doc_lengths):
    T, width = queries.shape
    heads = width // HD
    group = heads // KVH
    any_spec = pl.BlockSpec(memory_space=pl.ANY)
    vmem = pl.BlockSpec(memory_space=pltpu.VMEM)
    dma = pltpu.SemaphoreType.DMA
    return pl.pallas_call(
        functools.partial(kernel, n, doc_lengths.shape[0]),
        out_shape=(
            jax.ShapeDtypeStruct(queries.shape, BF16),
            jax.ShapeDtypeStruct(keys.shape, BF16),
            jax.ShapeDtypeStruct(values.shape, BF16),
        ),
        in_specs=[pl.BlockSpec(memory_space=pltpu.SMEM)] + [any_spec] * 6,
        out_specs=(any_spec, vmem, vmem),
        scratch_shapes=[
            pltpu.VMEM((T, width), BF16),
            pltpu.VMEM((T, width), BF16),
            pltpu.VMEM((T, width), BF16),
            pltpu.VMEM((heads, T), F32),
            pltpu.VMEM((2, T, KVH * HD), BF16),
            pltpu.VMEM((T, width), BF16),
            pltpu.VMEM((HD, heads * T), F32),
            pltpu.VMEM((KVH, 2, 5 * T, HD), BF16),
            pltpu.VMEM((5 * T, T), F32),
            pltpu.VMEM((heads, T), F32),
            pltpu.VMEM((5 * T, group * T), BF16),
            pltpu.VMEM((5 * T, group * T), BF16),
            pltpu.VMEM((HD, 5 * T), BF16),
            pltpu.VMEM((KVH, 2, T, HD), F32),
            pltpu.VMEM((2, KVH, 2, T, HD), F32),
            pltpu.VMEM((4, KVH, 2, T, HD), BF16),
            pltpu.VMEM((4, KVH, 2, T, HD), BF16),
            dma((6,)), dma((KVH,)),
            dma((4, KVH)), dma((4, KVH)), dma((4, KVH)), dma((4, KVH)),
        ],
        compiler_params=pltpu.CompilerParams(
            collective_id=0, has_side_effects=True, vmem_limit_bytes=60 * 1024 * 1024
        ),
        name="attention_grad",
    )(doc_lengths, queries, keys, values, outputs, out_grad, log_normalizer)


def solution(mesh):
    rows = P(("grp", "ctx"), None)
    in_specs = (rows,) * 5 + (P(None, ("grp", "ctx")), P("grp"))
    return jax.shard_map(
        functools.partial(body, mesh.shape["ctx"]),
        mesh=mesh, in_specs=in_specs, out_specs=(rows,) * 3, check_vma=False,
    )
```

```python
import functools
import math

import jax
import jax.numpy as jnp
from jax import lax
from jax.experimental import pallas as pl
from jax.experimental.pallas import tpu as pltpu
from jax.sharding import PartitionSpec as P

HD = 128
KVH = 4
SPAN = 4
EARLY = 2
LOG2E = 1.0 / math.log(2.0)
MESH = pl.DeviceIdType.MESH
F32 = jnp.float32
BF16 = jnp.bfloat16

CX, C, X, PB, M = range(5)


def nt(a, b):
    return lax.dot_general(a, b, (((1,), (1,)), ((), ())), preferred_element_type=F32)


def nn(a, b):
    return jnp.dot(a, b, preferred_element_type=F32)


def kernel(
    n, docs,
    doc_ref, q_hbm, k_hbm, v_hbm, o_hbm, do_hbm, ln_hbm,
    dq_hbm, dk_hbm, dv_hbm,
    q, o, do, ln, own, dq, dq_sum, dk_ref, dv_ref, kv, bias, rd, wbuf, gbuf, kt, acc_x, acc, bsend, brecv,
    load_sem, store_sem, fs_sem, fr_sem, bs_sem, br_sem,
):
    T = q_hbm.shape[0]
    heads = q_hbm.shape[1] // HD
    group = heads // KVH
    wide = group * HD
    inv_root = 1.0 / math.sqrt(HD)
    me = lax.axis_index("ctx")
    place = lax.rem(me, 4)
    x = place // 2
    c = lax.rem(place, 2)
    mate = me + 1 - 2 * c
    peer = me + 2 - 4 * x
    after = me + SPAN
    before = me - SPAN
    has_after = after < n
    has_before = before >= 0

    def load(i, src, dst):
        return pltpu.make_async_copy(src, dst, load_sem.at[i])

    loads_kv = [load(0, k_hbm, own.at[0]), load(1, v_hbm, own.at[1])]
    loads_rd = [load(2, do_hbm, do), load(3, o_hbm, o)]
    loads_q = [load(4, q_hbm, q), load(5, ln_hbm, ln)]
    for cp in loads_kv + loads_rd + loads_q:
        cp.start()

    barrier = pltpu.get_barrier_semaphore()
    pl.semaphore_signal(barrier, inc=1, device_id={"ctx": mate}, device_id_type=MESH)
    pl.semaphore_signal(barrier, inc=1, device_id={"ctx": peer}, device_id_type=MESH)

    @pl.when(has_after)
    def _():
        pl.semaphore_signal(barrier, inc=1, device_id={"ctx": after}, device_id_type=MESH)

    @pl.when(has_before)
    def _():
        pl.semaphore_signal(barrier, inc=1, device_id={"ctx": before}, device_id_type=MESH)

    for cp in loads_kv:
        cp.wait()
    for g in range(KVH):
        for a in range(2):
            kv[g, a, M * T:(M + 1) * T, :] = own[a, :, g * HD:(g + 1) * HD]

    @pl.when(jnp.logical_not(has_before))
    def _():
        kv[:, :, PB * T:(PB + 1) * T, :] = jnp.zeros((KVH, 2, T, HD), BF16)

    wait_for = 2 + jnp.where(has_after, 1, 0) + jnp.where(has_before, 1, 0)
    pl.semaphore_wait(barrier, wait_for)

    def fwd(kind, g, slot, target):
        row = slot * T if isinstance(slot, int) else pl.multiple_of(slot * T, T)
        return pltpu.make_async_remote_copy(
            src_ref=kv.at[g, :, pl.ds(row, T), :],
            dst_ref=kv.at[g, :, pl.ds(kind * T, T), :],
            send_sem=fs_sem.at[kind, g], recv_sem=fr_sem.at[kind, g],
            device_id={"ctx": target}, device_id_type=MESH,
        )

    def fwd_p(g):
        return fwd(PB, g, M, after)

    def fwd_x(g):
        return fwd(X, g, M - x, peer)

    def fwd_c(g):
        return fwd(C, g, M - c, mate)

    def fwd_cx(g):
        return fwd(CX, g, X, mate)

    @pl.when(has_after)
    def _():
        for g in range(KVH):
            fwd_p(g).start()

    @pl.when(x == 0)
    def _():
        for g in range(KVH):
            fwd_x(g).start()

    @pl.when(c == 0)
    def _():
        for g in range(KVH):
            fwd_c(g).start()

    def relay_p(g):
        @pl.when(has_before)
        def _():
            fwd_p(g).wait_recv()

        @pl.when(x == 1)
        def _():
            fwd_x(g).start()

        @pl.when(c == 1)
        def _():
            fwd_c(g).start()

    def relay_x(g):
        fwd_x(g).wait_recv()
        fwd_cx(g).start()

    def arrived(g):
        fwd_c(g).wait_recv()
        fwd_cx(g).wait_recv()

    t_row = lax.broadcasted_iota(jnp.int32, (1, T), 1)
    pos_row = me * T + t_row
    start_row = jnp.zeros((1, T), jnp.int32)
    end = jnp.int32(0)
    for i in range(docs):
        end = end + doc_ref[i]
        start_row = jnp.where(end <= pos_row, jnp.maximum(start_row, end), start_row)
    s_col = lax.broadcasted_iota(jnp.int32, (T, T), 0)
    t_col = lax.broadcasted_iota(jnp.int32, (T, T), 1)
    bases = (me - 1 - 2 * c, me - 3 + 2 * c, me - 2, me - SPAN, me)
    for slot, base in enumerate(bases):
        ok = base * T + s_col >= start_row
        if slot == PB:
            ok = ok & (s_col > t_col)
        if slot == M:
            ok = ok & (s_col <= t_col)
        bias[slot * T:(slot + 1) * T, :] = jnp.where(ok, 0.0, -1e30).astype(F32)

    for cp in loads_rd:
        cp.wait()
    pick = (
        lax.broadcasted_iota(jnp.int32, (16, wide), 1) // HD
        == lax.broadcasted_iota(jnp.int32, (16, wide), 0)
    )
    ones = jnp.where(pick, 1.0, 0.0).astype(BF16)
    for g in range(KVH):
        cols = slice(g * wide, (g + 1) * wide)
        prod = do[:, cols].astype(F32) * o[:, cols].astype(F32)
        high = prod.astype(BF16)
        low = (prod - high.astype(F32)).astype(BF16)
        rd[g * group:(g + 1) * group, :] = (nt(ones, high) + nt(ones, low))[:group]
    for cp in loads_q:
        cp.wait()

    def bwd(kind, g, target):
        return pltpu.make_async_remote_copy(
            src_ref=bsend.at[kind, g], dst_ref=brecv.at[kind, g],
            send_sem=bs_sem.at[kind, g], recv_sem=br_sem.at[kind, g],
            device_id={"ctx": target}, device_id_type=MESH,
        )

    def store(g):
        cols = pl.ds(g * wide, wide)
        return pltpu.make_async_copy(dq.at[:, cols], dq_hbm.at[:, cols], store_sem.at[g])

    def hop2(g):
        bwd(CX, g, mate).wait_recv()
        bsend[X, g] = (acc_x[g] + brecv[CX, g].astype(F32)).astype(BF16)
        bwd(X, g, peer).start()

    def hop3(g):
        bwd(C, g, mate).wait_recv()
        acc[c, g] = acc[c, g] + brecv[C, g].astype(F32)
        bwd(X, g, peer).wait_recv()
        acc[x, g] = acc[x, g] + brecv[X, g].astype(F32)

        @pl.when(has_before)
        def _():
            bsend[PB, g] = acc[1, g].astype(BF16)
            bwd(PB, g, before).start()

    def hop4(g):
        cols = slice(g * HD, (g + 1) * HD)

        @pl.when(has_after)
        def _():
            bwd(PB, g, before).wait_recv()
            total = acc[0, g] + brecv[PB, g].astype(F32)
            dk_ref[:, cols] = total[0].astype(BF16)
            dv_ref[:, cols] = total[1].astype(BF16)

        @pl.when(jnp.logical_not(has_after))
        def _():
            dk_ref[:, cols] = acc[0, g, 0].astype(BF16)
            dv_ref[:, cols] = acc[0, g, 1].astype(BF16)

    def pair_rows(ref, h):
        return jnp.concatenate(
            [ref[:, h * HD:(h + 1) * HD], ref[:, (h + 1) * HD:(h + 2) * HD]], axis=0
        )

    def pair_lanes(ref, h):
        return jnp.concatenate([ref[h:h + 1, :], ref[h + 1:h + 2, :]], axis=1)

    tri = jnp.concatenate([s_col <= t_col] * 2, axis=1)

    def tiles(g, first, last, start_sum, between=None):
        rows = slice(first * T, (last + 1) * T)
        k_rows = kv[g, 0, rows, :]
        v_rows = kv[g, 1, rows, :]
        kt[:, rows] = k_rows.T
        for p in range(group // 2):
            h = g * group + 2 * p
            st = nt(k_rows, pair_rows(q, h))
            gp = nt(v_rows, pair_rows(do, h))
            shift = pair_lanes(ln, h) * LOG2E
            dot_row = pair_lanes(rd, h)
            lanes = slice(p * 2 * T, (p + 1) * 2 * T)
            if first == PB and last == M:
                old, own_rows = slice(PB * T, M * T), slice(M * T, (M + 1) * T)
                b = jnp.maximum(bias[old, :], bias[own_rows, :])
                b = jnp.concatenate([b, b], axis=1)
                s_t = jnp.where(tri, st[T:], st[:T])
                g_t = jnp.where(tri, gp[T:], gp[:T])
                w = jnp.exp2(s_t * (inv_root * LOG2E) - shift + b)
                gs = w * (g_t - dot_row)
                wbuf[old, lanes] = jnp.where(tri, 0.0, w).astype(BF16)
                gbuf[old, lanes] = jnp.where(tri, 0.0, gs).astype(BF16)
                wbuf[own_rows, lanes] = jnp.where(tri, w, 0.0).astype(BF16)
                gbuf[own_rows, lanes] = jnp.where(tri, gs, 0.0).astype(BF16)
                slots = ()
            else:
                slots = range(first, last + 1)
            for slot in slots:
                part = slice((slot - first) * T, (slot - first + 1) * T)
                here = slice(slot * T, (slot + 1) * T)
                b = bias[here, :]
                b = jnp.concatenate([b, b], axis=1)
                w = jnp.exp2(st[part] * (inv_root * LOG2E) - shift + b)
                gs = w * (gp[part] - dot_row)
                wbuf[here, lanes] = w.astype(BF16)
                gbuf[here, lanes] = gs.astype(BF16)
            dqt = nn(kt[:, rows], gbuf[rows, lanes])
            sums = slice(h * T, (h + 2) * T)
            if start_sum:
                dq_sum[:, sums] = dqt
            elif last == X:
                dq_sum[:, sums] += dqt
            else:
                dqt = (dq_sum[:, sums] + dqt) * inv_root
                dq[:, h * HD:(h + 1) * HD] = dqt[:, :T].T.astype(BF16)
                dq[:, (h + 1) * HD:(h + 2) * HD] = dqt[:, T:].T.astype(BF16)
            if between is not None:
                between(p)
        dk = nn(gbuf[rows, :], stacked(q, g)) * inv_root
        dv = nn(wbuf[rows, :], stacked(do, g))
        return dk, dv

    def stacked(ref, g):
        return jnp.concatenate(
            [ref[:, (g * group + i) * HD:(g * group + i + 1) * HD] for i in range(group)], axis=0
        )

    for g in range(KVH):
        if g < EARLY:
            for a, part in enumerate(tiles(g, M, M, True)):
                acc[0, g, a] = part
        relay_p(g)

    relay_x(0)
    relay_x(1)
    for g in range(KVH):
        arrived(g)

        def between(p, g=g):
            if p == 0 and g + 2 < KVH:
                relay_x(g + 2)
            if p == 3 and g >= 1:
                hop2(g - 1)

        dk, dv = tiles(g, CX, X, g >= EARLY, between)
        for kind in (CX, C):
            bsend[kind, g, 0] = dk[kind * T:(kind + 1) * T].astype(BF16)
            bsend[kind, g, 1] = dv[kind * T:(kind + 1) * T].astype(BF16)
            bwd(kind, g, mate).start()
        acc_x[g, 0] = dk[X * T:]
        acc_x[g, 1] = dv[X * T:]

    for g in range(KVH):
        for a, part in enumerate(tiles(g, PB, PB if g < EARLY else M, False)):
            acc[1, g, a] = part[:T]
            if g >= EARLY:
                acc[0, g, a] = part[T:]
        store(g).start()
        if g == 0:
            hop2(KVH - 1)
        hop3(g)
    for g in range(KVH):
        hop4(g)
    last = [
        pltpu.make_async_copy(dk_ref, dk_hbm, store_sem.at[KVH]),
        pltpu.make_async_copy(dv_ref, dv_hbm, store_sem.at[KVH + 1]),
    ]
    for cp in last:
        cp.start()

    for cp in last:
        cp.wait()
    for g in range(KVH):
        store(g).wait()
        for kind, target in ((CX, mate), (C, mate), (X, peer)):
            bwd(kind, g, target).wait_send()
        fwd_x(g).wait_send()
        fwd_c(g).wait_send()
        fwd_cx(g).wait_send()

    @pl.when(has_after)
    def _():
        for g in range(KVH):
            fwd_p(g).wait_send()

    @pl.when(has_before)
    def _():
        for g in range(KVH):
            bwd(PB, g, before).wait_send()


def body(n, queries, keys, values, outputs, out_grad, log_normalizer, doc_lengths):
    T, width = queries.shape
    heads = width // HD
    group = heads // KVH
    any_spec = pl.BlockSpec(memory_space=pl.ANY)
    dma = pltpu.SemaphoreType.DMA
    return pl.pallas_call(
        functools.partial(kernel, n, doc_lengths.shape[0]),
        out_shape=(
            jax.ShapeDtypeStruct(queries.shape, BF16),
            jax.ShapeDtypeStruct(keys.shape, BF16),
            jax.ShapeDtypeStruct(values.shape, BF16),
        ),
        in_specs=[pl.BlockSpec(memory_space=pltpu.SMEM)] + [any_spec] * 6,
        out_specs=(any_spec,) * 3,
        scratch_shapes=[
            pltpu.VMEM((T, width), BF16),
            pltpu.VMEM((T, width), BF16),
            pltpu.VMEM((T, width), BF16),
            pltpu.VMEM((heads, T), F32),
            pltpu.VMEM((2, T, KVH * HD), BF16),
            pltpu.VMEM((T, width), BF16),
            pltpu.VMEM((HD, heads * T), F32),
            pltpu.VMEM((T, KVH * HD), BF16),
            pltpu.VMEM((T, KVH * HD), BF16),
            pltpu.VMEM((KVH, 2, 5 * T, HD), BF16),
            pltpu.VMEM((5 * T, T), F32),
            pltpu.VMEM((heads, T), F32),
            pltpu.VMEM((5 * T, group * T), BF16),
            pltpu.VMEM((5 * T, group * T), BF16),
            pltpu.VMEM((HD, 5 * T), BF16),
            pltpu.VMEM((KVH, 2, T, HD), F32),
            pltpu.VMEM((2, KVH, 2, T, HD), F32),
            pltpu.VMEM((4, KVH, 2, T, HD), BF16),
            pltpu.VMEM((4, KVH, 2, T, HD), BF16),
            dma((6,)), dma((KVH + 2,)),
            dma((4, KVH)), dma((4, KVH)), dma((4, KVH)), dma((4, KVH)),
        ],
        compiler_params=pltpu.CompilerParams(
            collective_id=0, has_side_effects=True, vmem_limit_bytes=60 * 1024 * 1024
        ),
        name="attention_grad",
    )(doc_lengths, queries, keys, values, outputs, out_grad, log_normalizer)


def solution(mesh):
    rows = P(("grp", "ctx"), None)
    in_specs = (rows,) * 5 + (P(None, ("grp", "ctx")), P("grp"))
    return jax.shard_map(
        functools.partial(body, mesh.shape["ctx"]),
        mesh=mesh, in_specs=in_specs, out_specs=(rows,) * 3, check_vma=False,
    )
```

```python
import functools
import math

import jax
import jax.numpy as jnp
from jax import lax
from jax.experimental import pallas as pl
from jax.experimental.pallas import tpu as pltpu
from jax.sharding import PartitionSpec as P

HD = 128
KVH = 4
SPAN = 4
EARLY = 2
LOG2E = 1.0 / math.log(2.0)
MESH = pl.DeviceIdType.MESH
F32 = jnp.float32
BF16 = jnp.bfloat16

CX, C, X, PB, M = range(5)


def nt(a, b):
    return lax.dot_general(a, b, (((1,), (1,)), ((), ())), preferred_element_type=F32)


def nn(a, b):
    return jnp.dot(a, b, preferred_element_type=F32)


def kernel(
    n, docs,
    doc_ref, q_hbm, k_hbm, v_hbm, o_hbm, do_hbm, ln_hbm,
    dq_hbm, dk_hbm, dv_hbm,
    q, o, do, ln, own, dq, dq_sum, dk_ref, dv_ref, kv, bias, rd, wbuf, gbuf, kt, acc_x, acc, bsend, brecv,
    load_sem, store_sem, fs_sem, fr_sem, bs_sem, br_sem,
):
    T = q_hbm.shape[0]
    heads = q_hbm.shape[1] // HD
    group = heads // KVH
    wide = group * HD
    inv_root = 1.0 / math.sqrt(HD)
    me = lax.axis_index("ctx")
    place = lax.rem(me, 4)
    x = place // 2
    c = lax.rem(place, 2)
    mate = me + 1 - 2 * c
    peer = me + 2 - 4 * x
    after = me + SPAN
    before = me - SPAN
    has_after = after < n
    has_before = before >= 0

    def load(i, src, dst):
        return pltpu.make_async_copy(src, dst, load_sem.at[i])

    loads_kv = [load(0, k_hbm, own.at[0]), load(1, v_hbm, own.at[1])]
    loads_rd = [load(2, do_hbm, do), load(3, o_hbm, o)]
    loads_q = [load(4, q_hbm, q), load(5, ln_hbm, ln)]
    for cp in loads_kv + loads_rd + loads_q:
        cp.start()

    barrier = pltpu.get_barrier_semaphore()
    pl.semaphore_signal(barrier, inc=1, device_id={"ctx": mate}, device_id_type=MESH)
    pl.semaphore_signal(barrier, inc=1, device_id={"ctx": peer}, device_id_type=MESH)

    @pl.when(has_after)
    def _():
        pl.semaphore_signal(barrier, inc=1, device_id={"ctx": after}, device_id_type=MESH)

    @pl.when(has_before)
    def _():
        pl.semaphore_signal(barrier, inc=1, device_id={"ctx": before}, device_id_type=MESH)

    for cp in loads_kv:
        cp.wait()
    for g in range(KVH):
        for a in range(2):
            kv[g, a, M * T:(M + 1) * T, :] = own[a, :, g * HD:(g + 1) * HD]

    @pl.when(jnp.logical_not(has_before))
    def _():
        kv[:, :, PB * T:(PB + 1) * T, :] = jnp.zeros((KVH, 2, T, HD), BF16)

    wait_for = 2 + jnp.where(has_after, 1, 0) + jnp.where(has_before, 1, 0)
    pl.semaphore_wait(barrier, wait_for)

    def fwd(kind, g, slot, target):
        row = slot * T if isinstance(slot, int) else pl.multiple_of(slot * T, T)
        return pltpu.make_async_remote_copy(
            src_ref=kv.at[g, :, pl.ds(row, T), :],
            dst_ref=kv.at[g, :, pl.ds(kind * T, T), :],
            send_sem=fs_sem.at[kind, g], recv_sem=fr_sem.at[kind, g],
            device_id={"ctx": target}, device_id_type=MESH,
        )

    def fwd_p(g):
        return fwd(PB, g, M, after)

    def fwd_x(g):
        return fwd(X, g, M - x, peer)

    def fwd_c(g):
        return fwd(C, g, M - c, mate)

    def fwd_cx(g):
        return fwd(CX, g, X, mate)

    @pl.when(has_after)
    def _():
        for g in range(KVH):
            fwd_p(g).start()

    @pl.when(x == 0)
    def _():
        for g in range(KVH):
            fwd_x(g).start()

    @pl.when(c == 0)
    def _():
        for g in range(KVH):
            fwd_c(g).start()

    def relay_p(g):
        @pl.when(has_before)
        def _():
            fwd_p(g).wait_recv()

        @pl.when(x == 1)
        def _():
            fwd_x(g).start()

        @pl.when(c == 1)
        def _():
            fwd_c(g).start()

    def relay_x(g):
        fwd_x(g).wait_recv()
        fwd_cx(g).start()

    def arrived(g):
        fwd_c(g).wait_recv()
        fwd_cx(g).wait_recv()

    t_row = lax.broadcasted_iota(jnp.int32, (1, T), 1)
    pos_row = me * T + t_row
    start_row = jnp.zeros((1, T), jnp.int32)
    end = jnp.int32(0)
    for i in range(docs):
        end = end + doc_ref[i]
        start_row = jnp.where(end <= pos_row, jnp.maximum(start_row, end), start_row)
    s_col = lax.broadcasted_iota(jnp.int32, (T, T), 0)
    t_col = lax.broadcasted_iota(jnp.int32, (T, T), 1)
    bases = (me - 1 - 2 * c, me - 3 + 2 * c, me - 2, me - SPAN, me)
    for slot, base in enumerate(bases):
        ok = base * T + s_col >= start_row
        if slot == PB:
            ok = ok & (s_col > t_col)
        if slot == M:
            ok = ok & (s_col <= t_col)
        bias[slot * T:(slot + 1) * T, :] = jnp.where(ok, 0.0, -1e30).astype(F32)

    for cp in loads_rd:
        cp.wait()
    pick = (
        lax.broadcasted_iota(jnp.int32, (16, wide), 1) // HD
        == lax.broadcasted_iota(jnp.int32, (16, wide), 0)
    )
    ones = jnp.where(pick, 1.0, 0.0).astype(BF16)
    for g in range(KVH):
        cols = slice(g * wide, (g + 1) * wide)
        prod = do[:, cols].astype(F32) * o[:, cols].astype(F32)
        high = prod.astype(BF16)
        low = (prod - high.astype(F32)).astype(BF16)
        rd[g * group:(g + 1) * group, :] = (nt(ones, high) + nt(ones, low))[:group]
    for cp in loads_q:
        cp.wait()

    def bwd(kind, g, target):
        return pltpu.make_async_remote_copy(
            src_ref=bsend.at[kind, g], dst_ref=brecv.at[kind, g],
            send_sem=bs_sem.at[kind, g], recv_sem=br_sem.at[kind, g],
            device_id={"ctx": target}, device_id_type=MESH,
        )

    def store(g):
        cols = pl.ds(g * wide, wide)
        return pltpu.make_async_copy(dq.at[:, cols], dq_hbm.at[:, cols], store_sem.at[g])

    def hop2(g):
        bwd(CX, g, mate).wait_recv()
        bsend[X, g] = (acc_x[g] + brecv[CX, g].astype(F32)).astype(BF16)
        bwd(X, g, peer).start()

    def hop3(g):
        bwd(C, g, mate).wait_recv()
        acc[c, g] = acc[c, g] + brecv[C, g].astype(F32)
        bwd(X, g, peer).wait_recv()
        acc[x, g] = acc[x, g] + brecv[X, g].astype(F32)

        @pl.when(has_before)
        def _():
            bsend[PB, g] = acc[1, g].astype(BF16)
            bwd(PB, g, before).start()

    def hop4(g):
        cols = slice(g * HD, (g + 1) * HD)

        @pl.when(has_after)
        def _():
            bwd(PB, g, before).wait_recv()
            total = acc[0, g] + brecv[PB, g].astype(F32)
            dk_ref[:, cols] = total[0].astype(BF16)
            dv_ref[:, cols] = total[1].astype(BF16)

        @pl.when(jnp.logical_not(has_after))
        def _():
            dk_ref[:, cols] = acc[0, g, 0].astype(BF16)
            dv_ref[:, cols] = acc[0, g, 1].astype(BF16)

    def pair_rows(ref, h):
        return jnp.concatenate(
            [ref[:, h * HD:(h + 1) * HD], ref[:, (h + 1) * HD:(h + 2) * HD]], axis=0
        )

    def pair_lanes(ref, h):
        return jnp.concatenate([ref[h:h + 1, :], ref[h + 1:h + 2, :]], axis=1)

    tri = jnp.concatenate([s_col <= t_col] * 2, axis=1)

    def tiles(g, first, last, start_sum, between=None):
        rows = slice(first * T, (last + 1) * T)
        k_rows = kv[g, 0, rows, :]
        v_rows = kv[g, 1, rows, :]
        kt[:, rows] = k_rows.T
        for p in range(group // 2):
            h = g * group + 2 * p
            st = nt(k_rows, pair_rows(q, h))
            gp = nt(v_rows, pair_rows(do, h))
            shift = pair_lanes(ln, h) * LOG2E
            dot_row = pair_lanes(rd, h)
            lanes = slice(p * 2 * T, (p + 1) * 2 * T)
            if first == PB and last == M:
                old, own_rows = slice(PB * T, M * T), slice(M * T, (M + 1) * T)
                b = jnp.maximum(bias[old, :], bias[own_rows, :])
                b = jnp.concatenate([b, b], axis=1)
                s_t = jnp.where(tri, st[T:], st[:T])
                g_t = jnp.where(tri, gp[T:], gp[:T])
                w = jnp.exp2(s_t * (inv_root * LOG2E) - shift + b)
                gs = w * (g_t - dot_row)
                wbuf[old, lanes] = jnp.where(tri, 0.0, w).astype(BF16)
                gbuf[old, lanes] = jnp.where(tri, 0.0, gs).astype(BF16)
                wbuf[own_rows, lanes] = jnp.where(tri, w, 0.0).astype(BF16)
                gbuf[own_rows, lanes] = jnp.where(tri, gs, 0.0).astype(BF16)
                slots = ()
            else:
                slots = range(first, last + 1)
            for slot in slots:
                part = slice((slot - first) * T, (slot - first + 1) * T)
                here = slice(slot * T, (slot + 1) * T)
                b = bias[here, :]
                b = jnp.concatenate([b, b], axis=1)
                w = jnp.exp2(st[part] * (inv_root * LOG2E) - shift + b)
                gs = w * (gp[part] - dot_row)
                wbuf[here, lanes] = w.astype(BF16)
                gbuf[here, lanes] = gs.astype(BF16)
            dqt = nn(kt[:, rows], gbuf[rows, lanes])
            sums = slice(h * T, (h + 2) * T)
            if start_sum:
                dq_sum[:, sums] = dqt
            elif last == X:
                dq_sum[:, sums] += dqt
            else:
                dqt = (dq_sum[:, sums] + dqt) * inv_root
                dq[:, h * HD:(h + 1) * HD] = dqt[:, :T].T.astype(BF16)
                dq[:, (h + 1) * HD:(h + 2) * HD] = dqt[:, T:].T.astype(BF16)
            if between is not None:
                between(p)
        dk = nn(gbuf[rows, :], stacked(q, g)) * inv_root
        dv = nn(wbuf[rows, :], stacked(do, g))
        return dk, dv

    def stacked(ref, g):
        return jnp.concatenate(
            [ref[:, (g * group + i) * HD:(g * group + i + 1) * HD] for i in range(group)], axis=0
        )

    for g in range(KVH):
        if g < EARLY:
            for a, part in enumerate(tiles(g, M, M, True)):
                acc[0, g, a] = part
        relay_p(g)

    relay_x(0)
    relay_x(1)
    for g in range(KVH):
        arrived(g)

        def between(p, g=g):
            if p == 0 and g + 2 < KVH:
                relay_x(g + 2)
            if p == 1 and g >= 1:
                hop2(g - 1)

        dk, dv = tiles(g, CX, X, g >= EARLY, between)
        for kind in (CX, C):
            bsend[kind, g, 0] = dk[kind * T:(kind + 1) * T].astype(BF16)
            bsend[kind, g, 1] = dv[kind * T:(kind + 1) * T].astype(BF16)
            bwd(kind, g, mate).start()
        acc_x[g, 0] = dk[X * T:]
        acc_x[g, 1] = dv[X * T:]

    for g in range(KVH):
        for a, part in enumerate(tiles(g, PB, PB if g < EARLY else M, False)):
            acc[1, g, a] = part[:T]
            if g >= EARLY:
                acc[0, g, a] = part[T:]
        store(g).start()
        if g == 0:
            hop2(KVH - 1)
        hop3(g)
    for g in range(KVH):
        hop4(g)
    last = [
        pltpu.make_async_copy(dk_ref, dk_hbm, store_sem.at[KVH]),
        pltpu.make_async_copy(dv_ref, dv_hbm, store_sem.at[KVH + 1]),
    ]
    for cp in last:
        cp.start()

    for cp in last:
        cp.wait()
    for g in range(KVH):
        store(g).wait()
        for kind, target in ((CX, mate), (C, mate), (X, peer)):
            bwd(kind, g, target).wait_send()
        fwd_x(g).wait_send()
        fwd_c(g).wait_send()
        fwd_cx(g).wait_send()

    @pl.when(has_after)
    def _():
        for g in range(KVH):
            fwd_p(g).wait_send()

    @pl.when(has_before)
    def _():
        for g in range(KVH):
            bwd(PB, g, before).wait_send()


def body(n, queries, keys, values, outputs, out_grad, log_normalizer, doc_lengths):
    T, width = queries.shape
    heads = width // HD
    group = heads // KVH
    any_spec = pl.BlockSpec(memory_space=pl.ANY)
    dma = pltpu.SemaphoreType.DMA
    return pl.pallas_call(
        functools.partial(kernel, n, doc_lengths.shape[0]),
        out_shape=(
            jax.ShapeDtypeStruct(queries.shape, BF16),
            jax.ShapeDtypeStruct(keys.shape, BF16),
            jax.ShapeDtypeStruct(values.shape, BF16),
        ),
        in_specs=[pl.BlockSpec(memory_space=pltpu.SMEM)] + [any_spec] * 6,
        out_specs=(any_spec,) * 3,
        scratch_shapes=[
            pltpu.VMEM((T, width), BF16),
            pltpu.VMEM((T, width), BF16),
            pltpu.VMEM((T, width), BF16),
            pltpu.VMEM((heads, T), F32),
            pltpu.VMEM((2, T, KVH * HD), BF16),
            pltpu.VMEM((T, width), BF16),
            pltpu.VMEM((HD, heads * T), F32),
            pltpu.VMEM((T, KVH * HD), BF16),
            pltpu.VMEM((T, KVH * HD), BF16),
            pltpu.VMEM((KVH, 2, 5 * T, HD), BF16),
            pltpu.VMEM((5 * T, T), F32),
            pltpu.VMEM((heads, T), F32),
            pltpu.VMEM((5 * T, group * T), BF16),
            pltpu.VMEM((5 * T, group * T), BF16),
            pltpu.VMEM((HD, 5 * T), BF16),
            pltpu.VMEM((KVH, 2, T, HD), F32),
            pltpu.VMEM((2, KVH, 2, T, HD), F32),
            pltpu.VMEM((4, KVH, 2, T, HD), BF16),
            pltpu.VMEM((4, KVH, 2, T, HD), BF16),
            dma((6,)), dma((KVH + 2,)),
            dma((4, KVH)), dma((4, KVH)), dma((4, KVH)), dma((4, KVH)),
        ],
        compiler_params=pltpu.CompilerParams(
            collective_id=0, has_side_effects=True, vmem_limit_bytes=60 * 1024 * 1024
        ),
        name="attention_grad",
    )(doc_lengths, queries, keys, values, outputs, out_grad, log_normalizer)


def solution(mesh):
    rows = P(("grp", "ctx"), None)
    in_specs = (rows,) * 5 + (P(None, ("grp", "ctx")), P("grp"))
    return jax.shard_map(
        functools.partial(body, mesh.shape["ctx"]),
        mesh=mesh, in_specs=in_specs, out_specs=(rows,) * 3, check_vma=False,
    )
```
